512 devices in a mesh: chan: 16 (over y, x), stretch: 32 (over z, core).
Axes of the slice: x: 4, y: 4, z: 16, core: 2. Of those that a mesh axis runs over, the one named last changes fastest.
Arguments:
- query_in: bfloat16 [16384, 8192], P('stretch', 'chan'), may hold values from -6 to 6
- key_in: bfloat16 [16384, 8192], P('stretch', 'chan'), may hold values from -6 to 6
- value_in: bfloat16 [16384, 8192], P('stretch', 'chan'), may hold values from -6 to 6
- contig_ids: int32 [16384], P('stretch'), may hold values from 0 to 3, never falling along the last dimension, each value on 1 to 8192 neighbouring positions
- short_taps: float32 [3, 7, 8192], P(None, None, 'chan'), may hold values from -2.4 to 2.4
- medium_taps: float32 [128, 8192], P(None, 'chan'), may hold values from -0.72 to 0.72
- decay_rate: float32 [8192], P('chan'), may hold values from 0.004 to 0.12
- skip_gain: float32 [8192], P('chan'), may hold values from -4 to 4
- out_weight: bfloat16 [8192, 8192], P('stretch', 'chan'), may hold values from -0.0625 to 0.0625
Outputs:
- layer_out: bfloat16 [16384, 8192], P('stretch', 'chan')
The draws below stay inside these ranges and needn't reach their ends.
Inputs may be any that keep to these rules, and one draw needn't show every extreme that they name: `contig_ids`: contig numbers never fall along the tokens; each of the 4 contigs holds 1 to 8192 tokens, and one holds exactly 8192.
All inputs are finite; a program needn't handle non-finite values.
Results may differ from the reference program's by a relative error of at most 0.0057.
Values may be sent and summed in bfloat16 or wider, within the bound.
No kernel may reach another device: no remote copies, remote signals or barrier semaphores. Data moves between devices by JAX's collectives and lax.ppermute only.
A program may use at most 64 MiB of HBM per device.

```python
import math
import jax
import jax.numpy as jnp
import numpy as np
from jax import lax

D = 8192
MEDIUM = 128
SHORT = 7
CONTIGS = 4
TOKENS = 16384
CONTIG_MOST = 8192


def steps_of(stream_key, dims, shards, smallest, high):
    def one(axis_at, shards_of):
        steps = jax.random.uniform(jax.random.fold_in(jax.random.fold_in(stream_key, 6), axis_at), (shards_of,), jnp.float32, smallest / len(shards), high / len(shards))
        return jnp.repeat(jnp.exp(steps), dims[axis_at] // shards_of).reshape((-1,) + (1,) * (len(dims) - axis_at - 1))

    level = one(*shards[0])
    for cut in shards[1:]:
        level = level * one(*cut)
    return level


def length_profile(number_of, total, most, lean):
    portions = [(1 << 20) // math.isqrt(rank ** lean) + 1 for rank in range(2, number_of + 1)]
    spare, counts = total - most - (number_of - 1), [1] * (number_of - 1)
    while spare > 0:
        candidates = [i for i in range(number_of - 1) if counts[i] < most]
        mass, left = sum([portions[i] for i in candidates]), spare
        for i in candidates:
            addition = min(most - counts[i], max(1, left * portions[i] // mass), spare)
            counts[i] = counts[i] + addition
            spare = spare - addition
    return np.array([most] + counts)


def uneven(stream_key, amount, total, reach, skew):
    if amount == 2:
        one = jax.random.randint(stream_key, (), max(1, total - reach), min(reach, total - 1) + 1)
        return jnp.stack([one, total - one])
    lengths = jnp.asarray(length_profile(amount, total, reach, skew), jnp.int32)
    twos = (amount - 1) // 2
    giver, taker = lengths[1:1 + 2 * twos:2], lengths[2:2 + 2 * twos:2]
    slack = jnp.minimum(giver - 1, reach - taker)
    moved = jax.random.randint(jax.random.fold_in(stream_key, 1), (twos,), 0, 1 << 20) % (slack + 1)
    lengths = lengths.at[1:1 + 2 * twos:2].set(giver - moved).at[2:2 + 2 * twos:2].set(taker + moved)
    return lengths[jax.random.permutation(jax.random.fold_in(stream_key, 2), amount)]


def noise(key, shape, width, reach, split=(), kind=jnp.bfloat16):
    values = jax.random.normal(key, shape, jnp.float32) * width
    if len(split) > 0:
        values = steps_of(key, shape, split, -0.22, 0.18) * values
    return jnp.clip(values, min=-reach, max=reach).astype(kind)


def setup_inputs(seed: int = 0) -> dict:
    streams_of = jax.random.split(jax.random.key(seed), 10)
    return {
        "query_in": noise(streams_of[0], (TOKENS, D), 1.0, 6.0, ((0, 32), (1, 16))),
        "key_in": noise(streams_of[1], (TOKENS, D), 1.0, 6.0, ((0, 32), (1, 16))),
        "value_in": noise(streams_of[2], (TOKENS, D), 1.0, 6.0, ((0, 32), (1, 16))),
        "contig_ids": jnp.searchsorted(jnp.cumsum(uneven(streams_of[3], CONTIGS, TOKENS, CONTIG_MOST, 2)), jnp.arange(TOKENS), side="right").astype(jnp.int32),
        "short_taps": noise(streams_of[4], (3, SHORT, D), 0.4, 2.4, ((2, 16),), jnp.float32),
        "medium_taps": noise(streams_of[5], (MEDIUM, D), 0.12, 0.72, ((1, 16),), jnp.float32),
        "decay_rate": jnp.clip(jnp.exp(math.log(0.12) - 3.4011973 * jax.random.uniform(streams_of[6], (D,), jnp.float32) ** steps_of(streams_of[6], (D,), ((0, 16),), -0.2, 0.2)), 0.004, 0.12),
        "skip_gain": noise(streams_of[7], (D,), 1.0, 4.0, ((0, 16),), jnp.float32),
        "out_weight": noise(streams_of[8], (D, D), D ** -0.5, 0.0625, ((0, 32), (1, 16))),
    }


def short_filter(source_rows, tap_table, reach_rows, length):
    summed = jnp.zeros(source_rows.shape, jnp.float32)
    for offset in range(SHORT):
        shifted = jnp.pad(source_rows, ((offset, 0), (0, 0)))[:length].astype(jnp.float32)
        summed = summed + jnp.where((reach_rows >= offset)[:, None], tap_table[offset][None, :] * shifted, 0.0)
    return summed


def reference(query_in, key_in, value_in, contig_ids, short_taps, medium_taps, decay_rate, skip_gain, out_weight):
    length = contig_ids.shape[0]
    position = jnp.arange(length, dtype=jnp.int32)
    prior_ids = jnp.concatenate([contig_ids[:1] - 1, contig_ids[:-1]])
    starts = jnp.where(contig_ids != prior_ids, position, 0).astype(jnp.int32)
    first_pos = lax.cummax(starts, axis=0)
    reach_rows = position - first_pos
    query_short = short_filter(query_in, short_taps[0], reach_rows, length)
    key_short = short_filter(key_in, short_taps[1], reach_rows, length)
    value_short = short_filter(value_in, short_taps[2], reach_rows, length)
    product = (key_short * value_short).astype(jnp.bfloat16)
    lag_steps = jnp.arange(MEDIUM, dtype=jnp.float32)
    filters = medium_taps * jnp.exp(-decay_rate[None, :] * lag_steps[:, None])
    padded = jnp.pad(product, ((MEDIUM - 1, 0), (0, 0)))

    def add_tap(offset, summed):
        begin = (MEDIUM - 1 - offset).astype(jnp.int32)
        shifted = lax.dynamic_slice_in_dim(padded, begin, length, 0).astype(jnp.float32)
        tap_row = lax.dynamic_slice_in_dim(filters, jnp.asarray(offset).astype(jnp.int32), 1, 0)
        return summed + jnp.where((reach_rows >= offset)[:, None], tap_row * shifted, 0.0)

    medium_out = lax.fori_loop(0, MEDIUM, add_tap, jnp.zeros(product.shape, jnp.float32))
    gated_out = (query_short * (medium_out + skip_gain[None, :] * product.astype(jnp.float32))).astype(jnp.bfloat16)
    return jnp.dot(gated_out, out_weight, preferred_element_type=jnp.float32).astype(jnp.bfloat16)
```

```python
import functools

import jax
import jax.numpy as jnp
from jax import lax
from jax.experimental import pallas as pl
from jax.experimental.pallas import tpu as pltpu
from jax.sharding import PartitionSpec as P

MEDIUM = 128
SHORT = 7
SIDE = 4
HALO = 144
HALF = 256
WINDOW = HALO + HALF
LEAD = 16
PRODUCTS = WINDOW - LEAD
TILE = 64
LANES = 128
OFFSETS = (0, -1, 1, 2)


def along_x(value, by):
    pairs = [
        (y * SIDE + x, y * SIDE + (x + by) % SIDE) for y in range(SIDE) for x in range(SIDE)
    ]
    return lax.ppermute(value, "chan", pairs)


def along_y(value, by):
    pairs = [
        (y * SIDE + x, (y + by) % SIDE * SIDE + x) for y in range(SIDE) for x in range(SIDE)
    ]
    return lax.ppermute(value, "chan", pairs)


def id_column(row):
    return jnp.broadcast_to(row, (LANES, LANES)).T


def filter_kernel(late, *refs):
    if late:
        halo_ref = halo_ids_ref = None
    else:
        halo_ref, halo_ids_ref, *refs = refs
    (query_ref, key_ref, value_ref, ids_ref, short_ref, medium_ref, decay_ref, skip_ref) = refs[:8]
    out_ref, query_f, key_f, value_f, ids_f, product_f, masked_f, taps_f, span = refs[8:]
    tiles = HALF // TILE

    @pl.when(pl.program_id(0) == 0)
    def _():
        own = [id_column(ids_ref[i : i + 1, :].astype(jnp.float32)) for i in range(4)]
        if late:
            ids_f[0:16, :] = own[0][112:128]
            for i in range(1, 4):
                ids_f[16 + 128 * (i - 1) : 16 + 128 * i, :] = own[i]
        else:
            before = [
                id_column(halo_ids_ref[0:1, 128 * i : 128 * i + 128].astype(jnp.float32))
                for i in (2, 3)
            ]
            ids_f[0:16, :] = before[0][112:128]
            ids_f[16:144, :] = before[1]
            ids_f[144:272, :] = own[0]
            ids_f[272:400, :] = own[1]
        for tile in range(tiles):
            rows = ids_f[HALO + TILE * tile : HALO + TILE * (tile + 1), :]
            span[2 * tile] = jnp.min(rows).astype(jnp.int32)
            span[2 * tile + 1] = jnp.max(rows).astype(jnp.int32)

    if late:
        first = 512 - WINDOW
        key_f[...] = key_ref[first:, :].astype(jnp.float32)
        value_f[...] = value_ref[first:, :].astype(jnp.float32)
        query_f[...] = query_ref[512 - HALF - 16 :, :].astype(jnp.float32)
    else:
        key_f[0:HALO, :] = halo_ref[0:HALO, :].astype(jnp.float32)
        key_f[HALO:, :] = key_ref[0:HALF, :].astype(jnp.float32)
        value_f[0:HALO, :] = halo_ref[HALO : 2 * HALO, :].astype(jnp.float32)
        value_f[HALO:, :] = value_ref[0:HALF, :].astype(jnp.float32)
        query_f[0:16, :] = halo_ref[2 * HALO : 2 * HALO + 16, :].astype(jnp.float32)
        query_f[16:, :] = query_ref[0:HALF, :].astype(jnp.float32)

    lag = lax.broadcasted_iota(jnp.int32, (MEDIUM, LANES), 0).astype(jnp.float32)
    taps_f[...] = medium_ref[...] * jnp.exp(-decay_ref[...] * lag)

    for tile in range(PRODUCTS // TILE):
        at = LEAD + TILE * tile
        here = ids_f[at : at + TILE, :]
        key_s = key_f[at : at + TILE, :] * short_ref[1, 0:1, :]
        value_s = value_f[at : at + TILE, :] * short_ref[2, 0:1, :]
        for j in range(1, SHORT):
            same = ids_f[at - j : at - j + TILE, :] == here
            key_s += jnp.where(same, key_f[at - j : at - j + TILE, :] * short_ref[1, j : j + 1, :], 0.0)
            value_s += jnp.where(
                same, value_f[at - j : at - j + TILE, :] * short_ref[2, j : j + 1, :], 0.0
            )
        product_f[TILE * tile : TILE * (tile + 1), :] = (
            (key_s * value_s).astype(jnp.bfloat16).astype(jnp.float32)
        )

    for tile in range(tiles):
        at = HALO + TILE * tile
        here = ids_f[at : at + TILE, :]
        query_s = query_f[16 + TILE * tile : 16 + TILE * (tile + 1), :] * short_ref[0, 0:1, :]
        for j in range(1, SHORT):
            same = ids_f[at - j : at - j + TILE, :] == here
            begin = 16 + TILE * tile - j
            query_s += jnp.where(
                same, query_f[begin : begin + TILE, :] * short_ref[0, j : j + 1, :], 0.0
            )

        def one_contig(contig, summed, tile=tile, here=here):
            contig = contig.astype(jnp.float32)
            reach = TILE + MEDIUM
            begin = TILE * tile
            masked_f[...] = jnp.where(
                ids_f[LEAD + begin : LEAD + begin + reach, :] == contig,
                product_f[begin : begin + reach, :],
                0.0,
            )
            total = jnp.zeros((TILE, LANES), jnp.float32)
            for r in range(8):
                shifted = masked_f[8 - r : 8 - r + reach - 8, :]
                for a in range(MEDIUM // 8):
                    total += (
                        taps_f[8 * a + r : 8 * a + r + 1, :]
                        * shifted[8 * (15 - a) : 8 * (15 - a) + TILE]
                    )
            return jnp.where(here == contig, total, summed)

        summed = lax.fori_loop(
            span[2 * tile],
            span[2 * tile + 1] + 1,
            one_contig,
            jnp.zeros((TILE, LANES), jnp.float32),
        )
        product = product_f[MEDIUM + TILE * tile : MEDIUM + TILE * (tile + 1), :]
        out_ref[TILE * tile : TILE * (tile + 1), :] = (
            query_s * (summed + skip_ref[...] * product)
        ).astype(jnp.bfloat16)


def gate(late, halo, query, key, value, ids, short_taps, medium_taps, decay, skip):
    channels = query.shape[1]
    whole = lambda rows: pl.BlockSpec((rows, LANES), lambda i: (0, i))
    specs = [whole(512)] * 3 + [
        pl.BlockSpec((4, LANES), lambda i: (0, 0)),
        pl.BlockSpec((3, SHORT, LANES), lambda i: (0, 0, i)),
        whole(MEDIUM),
        whole(1),
        whole(1),
    ]
    args = [query, key, value, ids, short_taps, medium_taps, decay, skip]
    if not late:
        ids_block = (2 * HALO + 16) // 16
        specs = [whole(halo.shape[0]), pl.BlockSpec((16, channels), lambda i: (ids_block, 0))] + specs
        args = [halo, halo] + args
    f32 = lambda rows: pltpu.VMEM((rows, LANES), jnp.float32)
    return pl.pallas_call(
        functools.partial(filter_kernel, late),
        grid=(channels // LANES,),
        out_shape=jax.ShapeDtypeStruct((HALF, channels), jnp.bfloat16),
        in_specs=specs,
        out_specs=pl.BlockSpec((HALF, LANES), lambda i: (0, i)),
        scratch_shapes=[
            f32(HALF + 16),
            f32(WINDOW),
            f32(WINDOW),
            f32(WINDOW),
            f32(PRODUCTS),
            f32(TILE + MEDIUM),
            f32(MEDIUM),
            pltpu.SMEM((2 * HALF // TILE,), jnp.int32),
        ],
        compiler_params=pltpu.CompilerParams(vmem_limit_bytes=24 << 20),
        cost_estimate=pl.CostEstimate(
            flops=2 * MEDIUM * HALF * channels * 4, bytes_accessed=2 << 20, transcendentals=65536
        ),
        name="gate_late" if late else "gate_early",
    )(*args)


def project_kernel(places, *refs):
    panels = refs[:8]
    weight, out_ref, blocks, weights, total, block_sem, weight_sem = refs[8:]
    copies = []
    for iy in range(SIDE):
        for ix in range(SIDE):
            at = SIDE * iy + ix
            mine = []
            mine.append(
                pltpu.make_async_copy(weight.at[places[at]], weights.at[at], weight_sem.at[at])
            )
            mine.append(
                pltpu.make_async_copy(
                    panels[iy].at[ix], blocks.at[at, pl.ds(HALF, HALF)], block_sem.at[2 * at]
                )
            )
            mine.append(
                pltpu.make_async_copy(
                    panels[4 + ix].at[iy], blocks.at[at, pl.ds(0, HALF)], block_sem.at[2 * at + 1]
                )
            )
            for copy in mine:
                copy.start()
            copies.append(mine)
    total[...] = jnp.zeros_like(total)
    for at in range(SIDE * SIDE):
        for copy in copies[at]:
            copy.wait()
        total[...] += jnp.dot(blocks[at], weights[at], preferred_element_type=jnp.float32)
    out_ref[...] = total[...].astype(jnp.bfloat16)


def project(late, early, weight):
    me = lax.axis_index("chan")
    y, x = me // SIDE, me % SIDE
    places = jnp.stack(
        [(y + oy) % SIDE * SIDE + (x + ox) % SIDE for oy in OFFSETS for ox in OFFSETS]
    ).astype(jnp.int32)
    columns = weight.shape[1]
    slots = SIDE * SIDE
    panels = [p.reshape(SIDE, HALF, -1) for p in (*late, *early)]
    depth = panels[0].shape[-1]
    hbm = pl.BlockSpec(memory_space=pl.ANY)
    return pl.pallas_call(
        project_kernel,
        out_shape=jax.ShapeDtypeStruct((2 * HALF, columns), jnp.bfloat16),
        in_specs=[pl.BlockSpec(memory_space=pltpu.SMEM)] + [hbm] * 9,
        out_specs=pl.BlockSpec(memory_space=pltpu.VMEM),
        scratch_shapes=[
            pltpu.VMEM((slots, 2 * HALF, depth), jnp.bfloat16),
            pltpu.VMEM((slots, depth, columns), jnp.bfloat16),
            pltpu.VMEM((2 * HALF, columns), jnp.float32),
            pltpu.SemaphoreType.DMA((2 * slots,)),
            pltpu.SemaphoreType.DMA((slots,)),
        ],
        compiler_params=pltpu.CompilerParams(vmem_limit_bytes=40 << 20),
        cost_estimate=pl.CostEstimate(
            flops=2 * 2 * HALF * slots * depth * columns, bytes_accessed=17 << 20, transcendentals=0
        ),
        name="project",
    )(places, *panels, weight.reshape(slots, depth, columns))


def body(
    query_in,
    key_in,
    value_in,
    contig_ids,
    short_taps,
    medium_taps,
    decay_rate,
    skip_gain,
    out_weight,
):
    tokens, channels = query_in.shape
    weight = lax.all_gather(out_weight, "stretch", axis=0, tiled=True)
    id_rows = jnp.broadcast_to(contig_ids.astype(jnp.bfloat16)[None, :], (16, tokens))
    pack = jnp.concatenate(
        [key_in[tokens - HALO :], value_in[tokens - HALO :], query_in[tokens - 16 :], id_rows]
    )
    devices = lax.axis_size("stretch")
    halo = lax.ppermute(pack, "stretch", [(i, i + 1) for i in range(devices - 1)])
    rest = (
        query_in,
        key_in,
        value_in,
        contig_ids.reshape(-1, LANES),
        short_taps,
        medium_taps,
        decay_rate[None, :],
        skip_gain[None, :],
    )
    late = gate(True, None, *rest)
    late_x = jnp.concatenate([late] + [along_x(late, -by) for by in OFFSETS[1:]])
    early = gate(False, halo, *rest)
    early_y = jnp.concatenate([early] + [along_y(early, -by) for by in OFFSETS[1:]])
    late_all = [late_x] + [along_y(late_x, -by) for by in OFFSETS[1:]]
    early_all = [early_y] + [along_x(early_y, -by) for by in OFFSETS[1:]]
    return project(late_all, early_all, weight)


def solution(mesh):
    placed = (
        P("stretch", "chan"),
        P("stretch", "chan"),
        P("stretch", "chan"),
        P("stretch"),
        P(None, None, "chan"),
        P(None, "chan"),
        P("chan"),
        P("chan"),
        P("stretch", "chan"),
    )
    return jax.shard_map(
        body, mesh=mesh, in_specs=placed, out_specs=P("stretch", "chan"), check_vma=False
    )
```

```python
import functools

import jax
import jax.numpy as jnp
from jax import lax
from jax.experimental import pallas as pl
from jax.experimental.pallas import tpu as pltpu
from jax.sharding import PartitionSpec as P

MEDIUM = 128
SHORT = 7
SIDE = 4
HALO = 144
HALF = 256
WINDOW = HALO + HALF
PACK = 2 * HALO + 16 + 16
LEAD = 16
PRODUCTS = WINDOW - LEAD
TILE = 64
LANES = 128
OFFSETS = (0, -1, 1, 2)


def first_way(value, by):
    return lax.ppermute(value, ("chan", "stretch"), moves(by, 0))


def second_way(value, by):
    return lax.ppermute(value, ("chan", "stretch"), moves(by, 1))


def moves(by, way):
    stretch = lax.axis_size("stretch")
    pairs = []
    for y in range(SIDE):
        for x in range(SIDE):
            for place in range(stretch):
                if place % 2 == way:
                    to = y * SIDE + (x + by) % SIDE
                else:
                    to = (y + by) % SIDE * SIDE + x
                pairs.append(((y * SIDE + x) * stretch + place, to * stretch + place))
    return pairs


def id_column(row):
    return jnp.broadcast_to(row, (LANES, LANES)).T


def filter_kernel(late, *refs):
    if late:
        halo_ref = halo_ids_ref = None
    else:
        halo_ref, halo_ids_ref, *refs = refs
    (query_ref, key_ref, value_ref, ids_ref, short_ref, medium_ref, decay_ref, skip_ref) = refs[:8]
    out_ref, query_f, key_f, value_f, ids_f, product_f, masked_f, taps_f, span = refs[8:]
    tiles = HALF // TILE

    @pl.when(pl.program_id(0) == 0)
    def _():
        own = [id_column(ids_ref[i : i + 1, :].astype(jnp.float32)) for i in range(4)]
        if late:
            ids_f[0:16, :] = own[0][112:128]
            for i in range(1, 4):
                ids_f[16 + 128 * (i - 1) : 16 + 128 * i, :] = own[i]
        else:
            before = [
                id_column(halo_ids_ref[0:1, 128 * i : 128 * i + 128].astype(jnp.float32))
                for i in (2, 3)
            ]
            ids_f[0:16, :] = before[0][112:128]
            ids_f[16:144, :] = before[1]
            ids_f[144:272, :] = own[0]
            ids_f[272:400, :] = own[1]
        for tile in range(tiles):
            rows = ids_f[HALO + TILE * tile : HALO + TILE * (tile + 1), :]
            span[2 * tile] = jnp.min(rows).astype(jnp.int32)
            span[2 * tile + 1] = jnp.max(rows).astype(jnp.int32)

    if late:
        first = 512 - WINDOW
        key_f[...] = key_ref[first:, :].astype(jnp.float32)
        value_f[...] = value_ref[first:, :].astype(jnp.float32)
        query_f[...] = query_ref[512 - HALF - 16 :, :].astype(jnp.float32)
    else:
        key_f[0:HALO, :] = halo_ref[0:HALO, :].astype(jnp.float32)
        key_f[HALO:, :] = key_ref[0:HALF, :].astype(jnp.float32)
        value_f[0:HALO, :] = halo_ref[HALO : 2 * HALO, :].astype(jnp.float32)
        value_f[HALO:, :] = value_ref[0:HALF, :].astype(jnp.float32)
        query_f[0:16, :] = halo_ref[2 * HALO : 2 * HALO + 16, :].astype(jnp.float32)
        query_f[16:, :] = query_ref[0:HALF, :].astype(jnp.float32)

    lag = lax.broadcasted_iota(jnp.int32, (MEDIUM, LANES), 0).astype(jnp.float32)
    taps_f[...] = medium_ref[...] * jnp.exp(-decay_ref[...] * lag)

    for tile in range(PRODUCTS // TILE):
        at = LEAD + TILE * tile
        here = ids_f[at : at + TILE, :]
        key_s = key_f[at : at + TILE, :] * short_ref[1, 0:1, :]
        value_s = value_f[at : at + TILE, :] * short_ref[2, 0:1, :]
        for j in range(1, SHORT):
            same = ids_f[at - j : at - j + TILE, :] == here
            key_s += jnp.where(same, key_f[at - j : at - j + TILE, :] * short_ref[1, j : j + 1, :], 0.0)
            value_s += jnp.where(
                same, value_f[at - j : at - j + TILE, :] * short_ref[2, j : j + 1, :], 0.0
            )
        product_f[TILE * tile : TILE * (tile + 1), :] = (
            (key_s * value_s).astype(jnp.bfloat16).astype(jnp.float32)
        )

    for tile in range(tiles):
        at = HALO + TILE * tile
        here = ids_f[at : at + TILE, :]
        query_s = query_f[16 + TILE * tile : 16 + TILE * (tile + 1), :] * short_ref[0, 0:1, :]
        for j in range(1, SHORT):
            same = ids_f[at - j : at - j + TILE, :] == here
            begin = 16 + TILE * tile - j
            query_s += jnp.where(
                same, query_f[begin : begin + TILE, :] * short_ref[0, j : j + 1, :], 0.0
            )

        def one_contig(contig, summed, tile=tile, here=here):
            contig = contig.astype(jnp.float32)
            reach = TILE + MEDIUM
            begin = TILE * tile
            masked_f[...] = jnp.where(
                ids_f[LEAD + begin : LEAD + begin + reach, :] == contig,
                product_f[begin : begin + reach, :],
                0.0,
            )
            total = jnp.zeros((TILE, LANES), jnp.float32)
            for r in range(8):
                shifted = masked_f[8 - r : 8 - r + reach - 8, :]
                for a in range(MEDIUM // 8):
                    total += (
                        taps_f[8 * a + r : 8 * a + r + 1, :]
                        * shifted[8 * (15 - a) : 8 * (15 - a) + TILE]
                    )
            return jnp.where(here == contig, total, summed)

        summed = lax.fori_loop(
            span[2 * tile],
            span[2 * tile + 1] + 1,
            one_contig,
            jnp.zeros((TILE, LANES), jnp.float32),
        )
        product = product_f[MEDIUM + TILE * tile : MEDIUM + TILE * (tile + 1), :]
        out_ref[TILE * tile : TILE * (tile + 1), :] = (
            query_s * (summed + skip_ref[...] * product)
        ).astype(jnp.bfloat16)


def pack_kernel(key, value, query, ids_ref, out, sem):
    copies = [
        pltpu.make_async_copy(key.at[512 - HALO : 512], out.at[0:HALO], sem.at[0]),
        pltpu.make_async_copy(value.at[512 - HALO : 512], out.at[HALO : 2 * HALO], sem.at[1]),
        pltpu.make_async_copy(
            query.at[512 - 16 : 512], out.at[2 * HALO : 2 * HALO + 16], sem.at[2]
        ),
    ]
    for copy in copies:
        copy.start()
    for i in range(4):
        row = ids_ref[i : i + 1, :].astype(jnp.float32)
        out[2 * HALO + 16 : PACK, LANES * i : LANES * (i + 1)] = jnp.broadcast_to(
            row, (16, LANES)
        ).astype(jnp.bfloat16)
    for copy in copies:
        copy.wait()


def pack_tail(key, value, query, ids):
    hbm = pl.BlockSpec(memory_space=pl.ANY)
    channels = key.shape[1]
    return pl.pallas_call(
        pack_kernel,
        out_shape=jax.ShapeDtypeStruct((PACK, channels), jnp.bfloat16),
        in_specs=[hbm, hbm, hbm, pl.BlockSpec(memory_space=pltpu.VMEM)],
        out_specs=pl.BlockSpec(memory_space=pltpu.VMEM),
        scratch_shapes=[pltpu.SemaphoreType.DMA((3,))],
        compiler_params=pltpu.CompilerParams(vmem_limit_bytes=60 << 20),
        cost_estimate=pl.CostEstimate(flops=0, bytes_accessed=700000, transcendentals=0),
        name="pack_tail",
    )(key, value, query, ids)


def gate(halo, query, key, value, ids, short_taps, medium_taps, decay, skip):
    late = halo is None
    channels = query.shape[1]
    whole = lambda rows: pl.BlockSpec((rows, LANES), lambda i: (0, i))
    specs = [whole(512)] * 3 + [
        pl.BlockSpec((4, LANES), lambda i: (0, 0)),
        pl.BlockSpec((3, SHORT, LANES), lambda i: (0, 0, i)),
        whole(MEDIUM),
        whole(1),
        whole(1),
    ]
    args = [query, key, value, ids, short_taps, medium_taps, decay, skip]
    if not late:
        ids_block = (2 * HALO + 16) // 16
        specs = [whole(PACK), pl.BlockSpec((16, channels), lambda i: (ids_block, 0))] + specs
        args = [halo, halo] + args
    f32 = lambda rows: pltpu.VMEM((rows, LANES), jnp.float32)
    return pl.pallas_call(
        functools.partial(filter_kernel, late),
        grid=(channels // LANES,),
        out_shape=jax.ShapeDtypeStruct((HALF, channels), jnp.bfloat16),
        in_specs=specs,
        out_specs=whole(HALF),
        scratch_shapes=[
            f32(HALF + 16),
            f32(WINDOW),
            f32(WINDOW),
            f32(WINDOW),
            f32(PRODUCTS),
            f32(TILE + MEDIUM),
            f32(MEDIUM),
            pltpu.SMEM((2 * HALF // TILE,), jnp.int32),
        ],
        compiler_params=pltpu.CompilerParams(vmem_limit_bytes=60 << 20),
        cost_estimate=pl.CostEstimate(
            flops=2 * MEDIUM * HALF * channels * 4, bytes_accessed=2 << 20, transcendentals=65536
        ),
        name="gate_late" if late else "gate_early",
    )(*args)


def project_kernel(places, *refs):
    lates, earlies = refs[:SIDE], refs[SIDE : 2 * SIDE]
    weight, out_ref, blocks, weights, total, block_sem, weight_sem = refs[2 * SIDE :]
    slots = SIDE * SIDE
    copies = []
    for at in range(slots):
        group, member = at // SIDE, at % SIDE
        copies.append(
            (
                pltpu.make_async_copy(
                    earlies[group].at[member], blocks.at[at, 0:HALF], block_sem.at[2 * at]
                ),
                pltpu.make_async_copy(
                    lates[group].at[member], blocks.at[at, HALF:], block_sem.at[2 * at + 1]
                ),
                pltpu.make_async_copy(weight.at[places[at]], weights.at[at], weight_sem.at[at]),
            )
        )
        for copy in copies[at]:
            copy.start()
    for at in range(slots):
        for copy in copies[at]:
            copy.wait()
        part = jnp.dot(blocks[at], weights[at], preferred_element_type=jnp.float32)
        if at == 0:
            total[...] = part
        elif at < slots - 1:
            total[...] += part
        else:
            out_ref[...] = (total[...] + part).astype(jnp.bfloat16)


def project(lates, earlies, weight):
    chan = lax.axis_index("chan")
    y, x = chan // SIDE, chan % SIDE
    core = lax.axis_index("stretch") % 2
    outer = jnp.repeat(jnp.array(OFFSETS, jnp.int32), SIDE)
    inner = jnp.tile(jnp.array(OFFSETS, jnp.int32), SIDE)
    oy = jnp.where(core == 0, outer, inner)
    ox = jnp.where(core == 0, inner, outer)
    places = (y + oy + SIDE) % SIDE * SIDE + (x + ox + SIDE) % SIDE
    slots = SIDE * SIDE
    columns = weight.shape[1]
    tokens, depth = 2 * HALF, lates[0].shape[2]
    hbm = pl.BlockSpec(memory_space=pl.ANY)
    return pl.pallas_call(
        project_kernel,
        out_shape=jax.ShapeDtypeStruct((tokens, columns), jnp.bfloat16),
        in_specs=[pl.BlockSpec(memory_space=pltpu.SMEM)] + [hbm] * 9,
        out_specs=pl.BlockSpec(memory_space=pltpu.VMEM),
        scratch_shapes=[
            pltpu.VMEM((slots, tokens, depth), jnp.bfloat16),
            pltpu.VMEM((slots, depth, columns), jnp.bfloat16),
            pltpu.VMEM((tokens, columns), jnp.float32),
            pltpu.SemaphoreType.DMA((2 * slots,)),
            pltpu.SemaphoreType.DMA((slots,)),
        ],
        compiler_params=pltpu.CompilerParams(vmem_limit_bytes=60 << 20),
        cost_estimate=pl.CostEstimate(
            flops=2 * tokens * slots * depth * columns, bytes_accessed=17 << 20, transcendentals=0
        ),
        name="project",
    )(places.astype(jnp.int32), *lates, *earlies, weight.reshape(slots, depth, columns))


def body(
    query_in,
    key_in,
    value_in,
    contig_ids,
    short_taps,
    medium_taps,
    decay_rate,
    skip_gain,
    out_weight,
):
    weight = lax.all_gather(out_weight, "stretch", axis=0, tiled=True)
    rest = (
        query_in,
        key_in,
        value_in,
        contig_ids.reshape(-1, LANES),
        short_taps,
        medium_taps,
        decay_rate[None, :],
        skip_gain[None, :],
    )
    devices = lax.axis_size("stretch")
    pack = pack_tail(key_in, value_in, query_in, rest[3])
    halo = lax.ppermute(pack, "stretch", [(i, i + 1) for i in range(devices - 1)])
    late = gate(None, *rest)
    late_line = [late] + [first_way(late, -by) for by in OFFSETS[1:]]
    early = gate(halo, *rest)
    late_line, early = lax.optimization_barrier((late_line, early))
    early_line = [early] + [first_way(early, -by) for by in OFFSETS[1:]]
    late_line, early_line = jnp.stack(late_line), jnp.stack(early_line)
    late_panels = [late_line] + [second_way(late_line, -by) for by in OFFSETS[1:]]
    early_panels = [early_line] + [second_way(early_line, -by) for by in OFFSETS[1:]]
    return project(late_panels, early_panels, weight)


def solution(mesh):
    placed = (
        P("stretch", "chan"),
        P("stretch", "chan"),
        P("stretch", "chan"),
        P("stretch"),
        P(None, None, "chan"),
        P(None, "chan"),
        P("chan"),
        P("chan"),
        P("stretch", "chan"),
    )
    return jax.shard_map(
        body, mesh=mesh, in_specs=placed, out_specs=P("stretch", "chan"), check_vma=False
    )
```

```python
import functools

import jax
import jax.numpy as jnp
from jax import lax
from jax.experimental import pallas as pl
from jax.experimental.pallas import tpu as pltpu
from jax.sharding import PartitionSpec as P

MEDIUM = 128
SHORT = 7
SIDE = 4
HALO = 144
HALF = 256
WINDOW = HALO + HALF
PACK = 2 * HALO + 16 + 16
LEAD = 16
PRODUCTS = WINDOW - LEAD
TILE = 64
LANES = 128
OFFSETS = (0, -1, 1, 2)


def first_way(value, by):
    return lax.ppermute(value, ("chan", "stretch"), moves(by, 0))


def second_way(value, by):
    return lax.ppermute(value, ("chan", "stretch"), moves(by, 1))


def moves(by, way):
    stretch = lax.axis_size("stretch")
    pairs = []
    for y in range(SIDE):
        for x in range(SIDE):
            for place in range(stretch):
                if place % 2 == way:
                    to = y * SIDE + (x + by) % SIDE
                else:
                    to = (y + by) % SIDE * SIDE + x
                pairs.append(((y * SIDE + x) * stretch + place, to * stretch + place))
    return pairs


def id_column(row):
    return jnp.broadcast_to(row, (LANES, LANES)).T


def filter_kernel(late, *refs):
    if late:
        halo_ref = halo_ids_ref = None
    else:
        _, halo_ref, halo_ids_ref, *refs = refs
    (query_ref, key_ref, value_ref, ids_ref, short_ref, medium_ref, decay_ref, skip_ref) = refs[:8]
    out_ref, query_f, key_f, value_f, ids_f, product_f, masked_f, taps_f, span = refs[8:]
    tiles = HALF // TILE

    @pl.when(pl.program_id(0) == 0)
    def _():
        own = [id_column(ids_ref[i : i + 1, :].astype(jnp.float32)) for i in range(4)]
        if late:
            ids_f[0:16, :] = own[0][112:128]
            for i in range(1, 4):
                ids_f[16 + 128 * (i - 1) : 16 + 128 * i, :] = own[i]
        else:
            before = [
                id_column(halo_ids_ref[0:1, 128 * i : 128 * i + 128].astype(jnp.float32))
                for i in (2, 3)
            ]
            ids_f[0:16, :] = before[0][112:128]
            ids_f[16:144, :] = before[1]
            ids_f[144:272, :] = own[0]
            ids_f[272:400, :] = own[1]
        for tile in range(tiles):
            rows = ids_f[HALO + TILE * tile : HALO + TILE * (tile + 1), :]
            span[2 * tile] = jnp.min(rows).astype(jnp.int32)
            span[2 * tile + 1] = jnp.max(rows).astype(jnp.int32)

    if late:
        first = 512 - WINDOW
        key_f[...] = key_ref[first:, :].astype(jnp.float32)
        value_f[...] = value_ref[first:, :].astype(jnp.float32)
        query_f[...] = query_ref[512 - HALF - 16 :, :].astype(jnp.float32)
    else:
        key_f[0:HALO, :] = halo_ref[0:HALO, :].astype(jnp.float32)
        key_f[HALO:, :] = key_ref[0:HALF, :].astype(jnp.float32)
        value_f[0:HALO, :] = halo_ref[HALO : 2 * HALO, :].astype(jnp.float32)
        value_f[HALO:, :] = value_ref[0:HALF, :].astype(jnp.float32)
        query_f[0:16, :] = halo_ref[2 * HALO : 2 * HALO + 16, :].astype(jnp.float32)
        query_f[16:, :] = query_ref[0:HALF, :].astype(jnp.float32)

    lag = lax.broadcasted_iota(jnp.int32, (MEDIUM, LANES), 0).astype(jnp.float32)
    taps_f[...] = medium_ref[...] * jnp.exp(-decay_ref[...] * lag)

    for tile in range(PRODUCTS // TILE):
        at = LEAD + TILE * tile
        here = ids_f[at : at + TILE, :]
        key_s = key_f[at : at + TILE, :] * short_ref[1, 0:1, :]
        value_s = value_f[at : at + TILE, :] * short_ref[2, 0:1, :]
        for j in range(1, SHORT):
            same = ids_f[at - j : at - j + TILE, :] == here
            key_s += jnp.where(same, key_f[at - j : at - j + TILE, :] * short_ref[1, j : j + 1, :], 0.0)
            value_s += jnp.where(
                same, value_f[at - j : at - j + TILE, :] * short_ref[2, j : j + 1, :], 0.0
            )
        product_f[TILE * tile : TILE * (tile + 1), :] = (
            (key_s * value_s).astype(jnp.bfloat16).astype(jnp.float32)
        )

    for tile in range(tiles):
        at = HALO + TILE * tile
        here = ids_f[at : at + TILE, :]
        query_s = query_f[16 + TILE * tile : 16 + TILE * (tile + 1), :] * short_ref[0, 0:1, :]
        for j in range(1, SHORT):
            same = ids_f[at - j : at - j + TILE, :] == here
            begin = 16 + TILE * tile - j
            query_s += jnp.where(
                same, query_f[begin : begin + TILE, :] * short_ref[0, j : j + 1, :], 0.0
            )

        def one_contig(contig, summed, tile=tile, here=here):
            contig = contig.astype(jnp.float32)
            reach = TILE + MEDIUM
            begin = TILE * tile
            masked_f[...] = jnp.where(
                ids_f[LEAD + begin : LEAD + begin + reach, :] == contig,
                product_f[begin : begin + reach, :],
                0.0,
            )
            total = jnp.zeros((TILE, LANES), jnp.float32)
            for r in range(8):
                shifted = masked_f[8 - r : 8 - r + reach - 8, :]
                for a in range(MEDIUM // 8):
                    total += (
                        taps_f[8 * a + r : 8 * a + r + 1, :]
                        * shifted[8 * (15 - a) : 8 * (15 - a) + TILE]
                    )
            return jnp.where(here == contig, total, summed)

        summed = lax.fori_loop(
            span[2 * tile],
            span[2 * tile + 1] + 1,
            one_contig,
            jnp.zeros((TILE, LANES), jnp.float32),
        )
        product = product_f[MEDIUM + TILE * tile : MEDIUM + TILE * (tile + 1), :]
        out_ref[TILE * tile : TILE * (tile + 1), :] = (
            query_s * (summed + skip_ref[...] * product)
        ).astype(jnp.bfloat16)


def pack_kernel(key, value, query, ids_ref, out, sem):
    copies = [
        pltpu.make_async_copy(key.at[512 - HALO : 512], out.at[0:HALO], sem.at[0]),
        pltpu.make_async_copy(value.at[512 - HALO : 512], out.at[HALO : 2 * HALO], sem.at[1]),
        pltpu.make_async_copy(
            query.at[512 - 16 : 512], out.at[2 * HALO : 2 * HALO + 16], sem.at[2]
        ),
    ]
    for copy in copies:
        copy.start()
    for i in range(4):
        row = ids_ref[i : i + 1, :].astype(jnp.float32)
        out[2 * HALO + 16 : PACK, LANES * i : LANES * (i + 1)] = jnp.broadcast_to(
            row, (16, LANES)
        ).astype(jnp.bfloat16)
    for copy in copies:
        copy.wait()


def pack_tail(key, value, query, ids):
    hbm = pl.BlockSpec(memory_space=pl.ANY)
    channels = key.shape[1]
    return pl.pallas_call(
        pack_kernel,
        out_shape=jax.ShapeDtypeStruct((PACK, channels), jnp.bfloat16),
        in_specs=[hbm, hbm, hbm, pl.BlockSpec(memory_space=pltpu.VMEM)],
        out_specs=pl.BlockSpec(memory_space=pltpu.VMEM),
        scratch_shapes=[pltpu.SemaphoreType.DMA((3,))],
        compiler_params=pltpu.CompilerParams(vmem_limit_bytes=60 << 20),
        cost_estimate=pl.CostEstimate(flops=0, bytes_accessed=700000, transcendentals=0),
        name="pack_tail",
    )(key, value, query, ids)


def gate(whole_gated, halo, query, key, value, ids, short_taps, medium_taps, decay, skip):
    late = whole_gated is None
    channels = query.shape[1]
    whole = lambda rows: pl.BlockSpec((rows, LANES), lambda i: (0, i))
    specs = [whole(512)] * 3 + [
        pl.BlockSpec((4, LANES), lambda i: (0, 0)),
        pl.BlockSpec((3, SHORT, LANES), lambda i: (0, 0, i)),
        whole(MEDIUM),
        whole(1),
        whole(1),
    ]
    args = [query, key, value, ids, short_taps, medium_taps, decay, skip]
    if not late:
        ids_block = (2 * HALO + 16) // 16
        specs = [pl.BlockSpec(memory_space=pl.ANY), whole(halo.shape[0]), pl.BlockSpec((16, channels), lambda i: (ids_block, 0))] + specs
        args = [whole_gated, halo, halo] + args
    f32 = lambda rows: pltpu.VMEM((rows, LANES), jnp.float32)
    return pl.pallas_call(
        functools.partial(filter_kernel, late),
        grid=(channels // LANES,),
        out_shape=jax.ShapeDtypeStruct((2 * HALF, channels), jnp.bfloat16),
        in_specs=specs,
        out_specs=pl.BlockSpec((HALF, LANES), lambda i: (int(late), i)),
        input_output_aliases={} if late else {0: 0},
        scratch_shapes=[
            f32(HALF + 16),
            f32(WINDOW),
            f32(WINDOW),
            f32(WINDOW),
            f32(PRODUCTS),
            f32(TILE + MEDIUM),
            f32(MEDIUM),
            pltpu.SMEM((2 * HALF // TILE,), jnp.int32),
        ],
        compiler_params=pltpu.CompilerParams(vmem_limit_bytes=60 << 20),
        cost_estimate=pl.CostEstimate(
            flops=2 * MEDIUM * HALF * channels * 4, bytes_accessed=2 << 20, transcendentals=65536
        ),
        name="gate_late" if late else "gate_early",
    )(*args)


def near_kernel(places, *refs):
    count = 2 * (SIDE - 1)
    panels = refs[:count]
    weight, total, far_weights, blocks, weights, block_sem, weight_sem = refs[count:]
    near = 2 * count
    copies = []
    for at in range(near):
        panel = panels[at // 2].at[at % 2]
        copies.append(
            (
                pltpu.make_async_copy(weight.at[places[at]], weights.at[at], weight_sem.at[at]),
                pltpu.make_async_copy(panel, blocks.at[at], block_sem.at[at]),
            )
        )
    later = [
        pltpu.make_async_copy(
            weight.at[places[near + i]], far_weights.at[i], weight_sem.at[near + i]
        )
        for i in range(SIDE)
    ]
    for pair in copies:
        for copy in pair:
            copy.start()
    for copy in later:
        copy.start()
    for at in range(near):
        for copy in copies[at]:
            copy.wait()
        part = jnp.dot(blocks[at], weights[at], preferred_element_type=jnp.float32)
        total[...] = part if at == 0 else total[...] + part
    for copy in later:
        copy.wait()


def far_kernel(total, weights, low, high, out_ref, blocks, summed, sem):
    copies = [
        pltpu.make_async_copy((low, high)[i // 2].at[i % 2], blocks.at[i], sem.at[i])
        for i in range(SIDE)
    ]
    for copy in copies:
        copy.start()
    for i in range(SIDE):
        copies[i].wait()
        part = jnp.dot(blocks[i], weights[i], preferred_element_type=jnp.float32)
        if i == 0:
            summed[...] = total[...] + part
        elif i < SIDE - 1:
            summed[...] += part
        else:
            out_ref[...] = (summed[...] + part).astype(jnp.bfloat16)


def project(near, far, weight):
    chan = lax.axis_index("chan")
    y, x = chan // SIDE, chan % SIDE
    core = lax.axis_index("stretch") % 2
    outer = jnp.repeat(jnp.array(OFFSETS, jnp.int32), SIDE)
    inner = jnp.tile(jnp.array(OFFSETS, jnp.int32), SIDE)
    oy = jnp.where(core == 0, outer, inner)
    ox = jnp.where(core == 0, inner, outer)
    places = (y + oy + SIDE) % SIDE * SIDE + (x + ox + SIDE) % SIDE
    slots = SIDE * SIDE
    columns = weight.shape[1]
    tokens, depth = near[0].shape[1:]
    hbm = pl.BlockSpec(memory_space=pl.ANY)
    vmem = pl.BlockSpec(memory_space=pltpu.VMEM)
    params = pltpu.CompilerParams(vmem_limit_bytes=54 << 20)
    cost = lambda blocks: pl.CostEstimate(
        flops=2 * tokens * blocks * depth * columns, bytes_accessed=blocks << 20, transcendentals=0
    )
    count = slots - SIDE
    total, weights = pl.pallas_call(
        near_kernel,
        out_shape=[
            pltpu.VMEM((tokens, columns), jnp.float32),
            pltpu.VMEM((SIDE, depth, columns), jnp.bfloat16),
        ],
        in_specs=[pl.BlockSpec(memory_space=pltpu.SMEM)] + [hbm] * (len(near) + 1),
        out_specs=[vmem, vmem],
        scratch_shapes=[
            pltpu.VMEM((count, tokens, depth), jnp.bfloat16),
            pltpu.VMEM((count, depth, columns), jnp.bfloat16),
            pltpu.SemaphoreType.DMA((count,)),
            pltpu.SemaphoreType.DMA((slots,)),
        ],
        compiler_params=params,
        cost_estimate=cost(count),
        name="project_near",
    )(places.astype(jnp.int32), *near, weight.reshape(slots, depth, columns))
    in_vmem = lambda value: pltpu.with_memory_space_constraint(value, pltpu.VMEM)
    return pl.pallas_call(
        far_kernel,
        out_shape=jax.ShapeDtypeStruct((tokens, columns), jnp.bfloat16),
        in_specs=[vmem, vmem, hbm, hbm],
        out_specs=vmem,
        scratch_shapes=[
            pltpu.VMEM((SIDE, tokens, depth), jnp.bfloat16),
            pltpu.VMEM((tokens, columns), jnp.float32),
            pltpu.SemaphoreType.DMA((SIDE,)),
        ],
        compiler_params=params,
        cost_estimate=cost(SIDE),
        name="project_far",
    )(in_vmem(total), in_vmem(weights), *far)


def body(
    query_in,
    key_in,
    value_in,
    contig_ids,
    short_taps,
    medium_taps,
    decay_rate,
    skip_gain,
    out_weight,
):
    weight = lax.all_gather(out_weight, "stretch", axis=0, tiled=True)
    rest = (
        query_in,
        key_in,
        value_in,
        contig_ids.reshape(-1, LANES),
        short_taps,
        medium_taps,
        decay_rate[None, :],
        skip_gain[None, :],
    )
    devices = lax.axis_size("stretch")
    pack = pack_tail(key_in, value_in, query_in, rest[3])
    halo = lax.ppermute(pack, "stretch", [(i, i + 1) for i in range(devices - 1)])
    gated = gate(None, None, *rest)
    gated = gate(gated, halo, *rest)
    line = [gated] + [first_way(gated, -by) for by in OFFSETS[1:]]
    low, high = jnp.stack(line[:2]), jnp.stack(line[2:])
    below_low = second_way(low, 1)
    above_high = second_way(high, -1)
    below_high = second_way(high, 1)
    above_low = second_way(low, -1)
    far_low = second_way(below_low, 1)
    far_high = second_way(above_high, -1)
    near = [low, high, below_low, below_high, above_low, above_high]
    return project(near, [far_low, far_high], weight)


def solution(mesh):
    placed = (
        P("stretch", "chan"),
        P("stretch", "chan"),
        P("stretch", "chan"),
        P("stretch"),
        P(None, None, "chan"),
        P(None, "chan"),
        P("chan"),
        P("chan"),
        P("stretch", "chan"),
    )
    return jax.shard_map(
        body, mesh=mesh, in_specs=placed, out_specs=P("stretch", "chan"), check_vma=False
    )
```

```python
import functools

import jax
import jax.numpy as jnp
from jax import lax
from jax.experimental import pallas as pl
from jax.experimental.pallas import tpu as pltpu
from jax.sharding import PartitionSpec as P

MEDIUM = 128
SHORT = 7
SIDE = 4
HALO = 144
HALF = 256
WINDOW = HALO + HALF
PACK = 2 * HALO + 16 + 16
LEAD = 16
PRODUCTS = WINDOW - LEAD
TILE = 64
LANES = 128
OFFSETS = (0, -1, 1, 2)


def first_way(value, by):
    return lax.ppermute(value, ("chan", "stretch"), moves(by, 0))


def second_way(value, by):
    return lax.ppermute(value, ("chan", "stretch"), moves(by, 1))


def moves(by, way):
    stretch = lax.axis_size("stretch")
    pairs = []
    for y in range(SIDE):
        for x in range(SIDE):
            for place in range(stretch):
                if place % 2 == way:
                    to = y * SIDE + (x + by) % SIDE
                else:
                    to = (y + by) % SIDE * SIDE + x
                pairs.append(((y * SIDE + x) * stretch + place, to * stretch + place))
    return pairs


def id_column(row):
    return jnp.broadcast_to(row, (LANES, LANES)).T


def filter_kernel(late, *refs):
    if late:
        halo_ref = halo_ids_ref = None
    else:
        _, halo_ref, halo_ids_ref, *refs = refs
    (query_ref, key_ref, value_ref, ids_ref, short_ref, medium_ref, decay_ref, skip_ref) = refs[:8]
    out_ref, query_f, key_f, value_f, ids_f, product_f, masked_f, taps_f, span = refs[8:]
    tiles = HALF // TILE

    @pl.when(pl.program_id(0) == 0)
    def _():
        own = [id_column(ids_ref[i : i + 1, :].astype(jnp.float32)) for i in range(4)]
        if late:
            ids_f[0:16, :] = own[0][112:128]
            for i in range(1, 4):
                ids_f[16 + 128 * (i - 1) : 16 + 128 * i, :] = own[i]
        else:
            before = [
                id_column(halo_ids_ref[0:1, 128 * i : 128 * i + 128].astype(jnp.float32))
                for i in (2, 3)
            ]
            ids_f[0:16, :] = before[0][112:128]
            ids_f[16:144, :] = before[1]
            ids_f[144:272, :] = own[0]
            ids_f[272:400, :] = own[1]
        for tile in range(tiles):
            rows = ids_f[HALO + TILE * tile : HALO + TILE * (tile + 1), :]
            span[2 * tile] = jnp.min(rows).astype(jnp.int32)
            span[2 * tile + 1] = jnp.max(rows).astype(jnp.int32)

    if late:
        first = 512 - WINDOW
        key_f[...] = key_ref[first:, :].astype(jnp.float32)
        value_f[...] = value_ref[first:, :].astype(jnp.float32)
        query_f[...] = query_ref[512 - HALF - 16 :, :].astype(jnp.float32)
    else:
        key_f[0:HALO, :] = halo_ref[0:HALO, :].astype(jnp.float32)
        key_f[HALO:, :] = key_ref[0:HALF, :].astype(jnp.float32)
        value_f[0:HALO, :] = halo_ref[HALO : 2 * HALO, :].astype(jnp.float32)
        value_f[HALO:, :] = value_ref[0:HALF, :].astype(jnp.float32)
        query_f[0:16, :] = halo_ref[2 * HALO : 2 * HALO + 16, :].astype(jnp.float32)
        query_f[16:, :] = query_ref[0:HALF, :].astype(jnp.float32)

    lag = lax.broadcasted_iota(jnp.int32, (MEDIUM, LANES), 0).astype(jnp.float32)
    taps_f[...] = medium_ref[...] * jnp.exp(-decay_ref[...] * lag)

    for tile in range(PRODUCTS // TILE):
        at = LEAD + TILE * tile
        here = ids_f[at : at + TILE, :]
        key_s = key_f[at : at + TILE, :] * short_ref[1, 0:1, :]
        value_s = value_f[at : at + TILE, :] * short_ref[2, 0:1, :]
        for j in range(1, SHORT):
            same = ids_f[at - j : at - j + TILE, :] == here
            key_s += jnp.where(same, key_f[at - j : at - j + TILE, :] * short_ref[1, j : j + 1, :], 0.0)
            value_s += jnp.where(
                same, value_f[at - j : at - j + TILE, :] * short_ref[2, j : j + 1, :], 0.0
            )
        product_f[TILE * tile : TILE * (tile + 1), :] = (
            (key_s * value_s).astype(jnp.bfloat16).astype(jnp.float32)
        )

    for tile in range(tiles):
        at = HALO + TILE * tile
        here = ids_f[at : at + TILE, :]
        query_s = query_f[16 + TILE * tile : 16 + TILE * (tile + 1), :] * short_ref[0, 0:1, :]
        for j in range(1, SHORT):
            same = ids_f[at - j : at - j + TILE, :] == here
            begin = 16 + TILE * tile - j
            query_s += jnp.where(
                same, query_f[begin : begin + TILE, :] * short_ref[0, j : j + 1, :], 0.0
            )

        def one_contig(contig, summed, tile=tile, here=here):
            contig = contig.astype(jnp.float32)
            reach = TILE + MEDIUM
            begin = TILE * tile
            masked_f[...] = jnp.where(
                ids_f[LEAD + begin : LEAD + begin + reach, :] == contig,
                product_f[begin : begin + reach, :],
                0.0,
            )
            total = jnp.zeros((TILE, LANES), jnp.float32)
            for r in range(8):
                shifted = masked_f[8 - r : 8 - r + reach - 8, :]
                for a in range(MEDIUM // 8):
                    total += (
                        taps_f[8 * a + r : 8 * a + r + 1, :]
                        * shifted[8 * (15 - a) : 8 * (15 - a) + TILE]
                    )
            return jnp.where(here == contig, total, summed)

        summed = lax.fori_loop(
            span[2 * tile],
            span[2 * tile + 1] + 1,
            one_contig,
            jnp.zeros((TILE, LANES), jnp.float32),
        )
        product = product_f[MEDIUM + TILE * tile : MEDIUM + TILE * (tile + 1), :]
        out_ref[TILE * tile : TILE * (tile + 1), :] = (
            query_s * (summed + skip_ref[...] * product)
        ).astype(jnp.bfloat16)


def pack_kernel(key, value, query, ids_ref, out, sem):
    copies = [
        pltpu.make_async_copy(key.at[512 - HALO : 512], out.at[0:HALO], sem.at[0]),
        pltpu.make_async_copy(value.at[512 - HALO : 512], out.at[HALO : 2 * HALO], sem.at[1]),
        pltpu.make_async_copy(
            query.at[512 - 16 : 512], out.at[2 * HALO : 2 * HALO + 16], sem.at[2]
        ),
    ]
    for copy in copies:
        copy.start()
    for i in range(4):
        row = ids_ref[i : i + 1, :].astype(jnp.float32)
        out[2 * HALO + 16 : PACK, LANES * i : LANES * (i + 1)] = jnp.broadcast_to(
            row, (16, LANES)
        ).astype(jnp.bfloat16)
    for copy in copies:
        copy.wait()


def pack_tail(key, value, query, ids):
    hbm = pl.BlockSpec(memory_space=pl.ANY)
    channels = key.shape[1]
    return pl.pallas_call(
        pack_kernel,
        out_shape=jax.ShapeDtypeStruct((PACK, channels), jnp.bfloat16),
        in_specs=[hbm, hbm, hbm, pl.BlockSpec(memory_space=pltpu.VMEM)],
        out_specs=pl.BlockSpec(memory_space=pltpu.VMEM),
        scratch_shapes=[pltpu.SemaphoreType.DMA((3,))],
        compiler_params=pltpu.CompilerParams(vmem_limit_bytes=60 << 20),
        cost_estimate=pl.CostEstimate(flops=0, bytes_accessed=700000, transcendentals=0),
        name="pack_tail",
    )(key, value, query, ids)


def gate(whole_gated, halo, query, key, value, ids, short_taps, medium_taps, decay, skip):
    late = whole_gated is None
    channels = query.shape[1]
    whole = lambda rows: pl.BlockSpec((rows, LANES), lambda i: (0, i))
    specs = [whole(512)] * 3 + [
        pl.BlockSpec((4, LANES), lambda i: (0, 0)),
        pl.BlockSpec((3, SHORT, LANES), lambda i: (0, 0, i)),
        whole(MEDIUM),
        whole(1),
        whole(1),
    ]
    args = [query, key, value, ids, short_taps, medium_taps, decay, skip]
    if not late:
        ids_block = (2 * HALO + 16) // 16
        specs = [pl.BlockSpec(memory_space=pl.ANY), whole(halo.shape[0]), pl.BlockSpec((16, channels), lambda i: (ids_block, 0))] + specs
        args = [whole_gated, halo, halo] + args
    f32 = lambda rows: pltpu.VMEM((rows, LANES), jnp.float32)
    return pl.pallas_call(
        functools.partial(filter_kernel, late),
        grid=(channels // LANES,),
        out_shape=jax.ShapeDtypeStruct((2 * HALF, channels), jnp.bfloat16),
        in_specs=specs,
        out_specs=pl.BlockSpec((HALF, LANES), lambda i: (int(late), i)),
        input_output_aliases={} if late else {0: 0},
        scratch_shapes=[
            f32(HALF + 16),
            f32(WINDOW),
            f32(WINDOW),
            f32(WINDOW),
            f32(PRODUCTS),
            f32(TILE + MEDIUM),
            f32(MEDIUM),
            pltpu.SMEM((2 * HALF // TILE,), jnp.int32),
        ],
        compiler_params=pltpu.CompilerParams(vmem_limit_bytes=60 << 20),
        cost_estimate=pl.CostEstimate(
            flops=2 * MEDIUM * HALF * channels * 4, bytes_accessed=2 << 20, transcendentals=65536
        ),
        name="gate_late" if late else "gate_early",
    )(*args)


def near_kernel(places, *refs):
    count = 2 * SIDE - 1
    panels = refs[:count]
    weight, total, far_weights, blocks, weights, block_sem, weight_sem = refs[count:]
    near = 2 * count
    copies = []
    for at in range(near):
        panel = panels[at // 2].at[at % 2]
        copies.append(
            (
                pltpu.make_async_copy(weight.at[places[at]], weights.at[at], weight_sem.at[at]),
                pltpu.make_async_copy(panel, blocks.at[at], block_sem.at[at]),
            )
        )
    later = [
        pltpu.make_async_copy(
            weight.at[places[near + i]], far_weights.at[i], weight_sem.at[near + i]
        )
        for i in range(2)
    ]
    for pair in copies:
        for copy in pair:
            copy.start()
    for copy in later:
        copy.start()
    for at in range(near):
        for copy in copies[at]:
            copy.wait()
        part = jnp.dot(blocks[at], weights[at], preferred_element_type=jnp.float32)
        total[...] = part if at == 0 else total[...] + part
    for copy in later:
        copy.wait()


def far_kernel(total, weights, panel, out_ref, blocks, rounded, sem, out_sem):
    copies = [pltpu.make_async_copy(panel.at[i], blocks.at[i], sem.at[i]) for i in range(2)]
    for copy in copies:
        copy.start()
    for copy in copies:
        copy.wait()
    tokens = total.shape[0]
    gives = []
    for half in range(2):
        rows = slice(tokens // 2 * half, tokens // 2 * (half + 1))
        summed = total[rows]
        for i in range(2):
            summed += jnp.dot(blocks[i, rows], weights[i], preferred_element_type=jnp.float32)
        rounded[rows] = summed.astype(jnp.bfloat16)
        gives.append(pltpu.make_async_copy(rounded.at[rows], out_ref.at[rows], out_sem.at[half]))
        gives[half].start()
    for give in gives:
        give.wait()


def project(near, far, weight):
    chan = lax.axis_index("chan")
    y, x = chan // SIDE, chan % SIDE
    core = lax.axis_index("stretch") % 2
    outer = jnp.repeat(jnp.array(OFFSETS, jnp.int32), SIDE)
    inner = jnp.tile(jnp.array(OFFSETS, jnp.int32), SIDE)
    oy = jnp.where(core == 0, outer, inner)
    ox = jnp.where(core == 0, inner, outer)
    places = (y + oy + SIDE) % SIDE * SIDE + (x + ox + SIDE) % SIDE
    slots = SIDE * SIDE
    columns = weight.shape[1]
    tokens, depth = near[0].shape[1:]
    hbm = pl.BlockSpec(memory_space=pl.ANY)
    vmem = pl.BlockSpec(memory_space=pltpu.VMEM)
    params = pltpu.CompilerParams(vmem_limit_bytes=54 << 20)
    cost = lambda blocks: pl.CostEstimate(
        flops=2 * tokens * blocks * depth * columns, bytes_accessed=blocks << 20, transcendentals=0
    )
    count = slots - 2
    total, weights = pl.pallas_call(
        near_kernel,
        out_shape=[
            pltpu.VMEM((tokens, columns), jnp.float32),
            pltpu.VMEM((2, depth, columns), jnp.bfloat16),
        ],
        in_specs=[pl.BlockSpec(memory_space=pltpu.SMEM)] + [hbm] * (len(near) + 1),
        out_specs=[vmem, vmem],
        scratch_shapes=[
            pltpu.VMEM((count, tokens, depth), jnp.bfloat16),
            pltpu.VMEM((count, depth, columns), jnp.bfloat16),
            pltpu.SemaphoreType.DMA((count,)),
            pltpu.SemaphoreType.DMA((slots,)),
        ],
        compiler_params=params,
        cost_estimate=cost(count),
        name="project_near",
    )(places.astype(jnp.int32), *near, weight.reshape(slots, depth, columns))
    in_vmem = lambda value: pltpu.with_memory_space_constraint(value, pltpu.VMEM)
    return pl.pallas_call(
        far_kernel,
        out_shape=jax.ShapeDtypeStruct((tokens, columns), jnp.bfloat16),
        in_specs=[vmem, vmem, hbm],
        out_specs=hbm,
        scratch_shapes=[
            pltpu.VMEM((2, tokens, depth), jnp.bfloat16),
            pltpu.VMEM((tokens, columns), jnp.bfloat16),
            pltpu.SemaphoreType.DMA((2,)),
            pltpu.SemaphoreType.DMA((2,)),
        ],
        compiler_params=params,
        cost_estimate=cost(2),
        name="project_far",
    )(in_vmem(total), in_vmem(weights), far)


def body(
    query_in,
    key_in,
    value_in,
    contig_ids,
    short_taps,
    medium_taps,
    decay_rate,
    skip_gain,
    out_weight,
):
    weight = lax.all_gather(out_weight, "stretch", axis=0, tiled=True)
    rest = (
        query_in,
        key_in,
        value_in,
        contig_ids.reshape(-1, LANES),
        short_taps,
        medium_taps,
        decay_rate[None, :],
        skip_gain[None, :],
    )
    devices = lax.axis_size("stretch")
    pack = pack_tail(key_in, value_in, query_in, rest[3])
    halo = lax.ppermute(pack, "stretch", [(i, i + 1) for i in range(devices - 1)])
    gated = gate(None, None, *rest)
    gated = gate(gated, halo, *rest)
    line = [gated] + [first_way(gated, -by) for by in OFFSETS[1:]]
    low, high = jnp.stack(line[:2]), jnp.stack(line[2:])
    below_low = second_way(low, 1)
    above_high = second_way(high, -1)
    below_high = second_way(high, 1)
    above_low = second_way(low, -1)
    far_low = second_way(below_low, 1)
    far_high = second_way(above_high, -1)
    near = [low, high, below_low, below_high, above_low, above_high, far_low]
    return project(near, far_high, weight)


def solution(mesh):
    placed = (
        P("stretch", "chan"),
        P("stretch", "chan"),
        P("stretch", "chan"),
        P("stretch"),
        P(None, None, "chan"),
        P(None, "chan"),
        P("chan"),
        P("chan"),
        P("stretch", "chan"),
    )
    return jax.shard_map(
        body, mesh=mesh, in_specs=placed, out_specs=P("stretch", "chan"), check_vma=False
    )
```

```python
import functools

import jax
import jax.numpy as jnp
from jax import lax
from jax.experimental import pallas as pl
from jax.experimental.pallas import tpu as pltpu
from jax.sharding import PartitionSpec as P

MEDIUM = 128
SHORT = 7
SIDE = 4
HALO = 144
HALF = 256
WINDOW = HALO + HALF
PACK = 2 * HALO + 16 + 16
LEAD = 16
PRODUCTS = WINDOW - LEAD
TILE = 64
LANES = 128
OFFSETS = (0, -1, 1, 2)


def first_way(value, by):
    return lax.ppermute(value, ("chan", "stretch"), moves(by, 0))


def second_way(value, by):
    return lax.ppermute(value, ("chan", "stretch"), moves(by, 1))


def moves(by, way):
    stretch = lax.axis_size("stretch")
    pairs = []
    for y in range(SIDE):
        for x in range(SIDE):
            for place in range(stretch):
                if place % 2 == way:
                    to = y * SIDE + (x + by) % SIDE
                else:
                    to = (y + by) % SIDE * SIDE + x
                pairs.append(((y * SIDE + x) * stretch + place, to * stretch + place))
    return pairs


def id_column(row):
    return jnp.broadcast_to(row, (LANES, LANES)).T


def filter_kernel(late, *refs):
    if late:
        halo_ref = halo_ids_ref = None
    else:
        _, halo_ref, halo_ids_ref, *refs = refs
    (query_ref, key_ref, value_ref, ids_ref, short_ref, medium_ref, decay_ref, skip_ref) = refs[:8]
    out_ref, query_f, key_f, value_f, ids_f, product_f, masked_f, taps_f, span = refs[8:]
    tiles = HALF // TILE

    @pl.when(pl.program_id(0) == 0)
    def _():
        own = [id_column(ids_ref[i : i + 1, :].astype(jnp.float32)) for i in range(4)]
        if late:
            ids_f[0:16, :] = own[0][112:128]
            for i in range(1, 4):
                ids_f[16 + 128 * (i - 1) : 16 + 128 * i, :] = own[i]
        else:
            before = [
                id_column(halo_ids_ref[0:1, 128 * i : 128 * i + 128].astype(jnp.float32))
                for i in (2, 3)
            ]
            ids_f[0:16, :] = before[0][112:128]
            ids_f[16:144, :] = before[1]
            ids_f[144:272, :] = own[0]
            ids_f[272:400, :] = own[1]
        for tile in range(tiles):
            rows = ids_f[HALO + TILE * tile : HALO + TILE * (tile + 1), :]
            span[2 * tile] = jnp.min(rows).astype(jnp.int32)
            span[2 * tile + 1] = jnp.max(rows).astype(jnp.int32)

    if late:
        first = 512 - WINDOW
        key_f[...] = key_ref[first:, :].astype(jnp.float32)
        value_f[...] = value_ref[first:, :].astype(jnp.float32)
        query_f[...] = query_ref[512 - HALF - 16 :, :].astype(jnp.float32)
    else:
        key_f[0:HALO, :] = halo_ref[0:HALO, :].astype(jnp.float32)
        key_f[HALO:, :] = key_ref[0:HALF, :].astype(jnp.float32)
        value_f[0:HALO, :] = halo_ref[HALO : 2 * HALO, :].astype(jnp.float32)
        value_f[HALO:, :] = value_ref[0:HALF, :].astype(jnp.float32)
        query_f[0:16, :] = halo_ref[2 * HALO : 2 * HALO + 16, :].astype(jnp.float32)
        query_f[16:, :] = query_ref[0:HALF, :].astype(jnp.float32)

    lag = lax.broadcasted_iota(jnp.int32, (MEDIUM, LANES), 0).astype(jnp.float32)
    taps_f[...] = medium_ref[...] * jnp.exp(-decay_ref[...] * lag)

    for tile in range(PRODUCTS // TILE):
        at = LEAD + TILE * tile
        here = ids_f[at : at + TILE, :]
        key_s = key_f[at : at + TILE, :] * short_ref[1, 0:1, :]
        value_s = value_f[at : at + TILE, :] * short_ref[2, 0:1, :]
        for j in range(1, SHORT):
            same = ids_f[at - j : at - j + TILE, :] == here
            key_s += jnp.where(same, key_f[at - j : at - j + TILE, :] * short_ref[1, j : j + 1, :], 0.0)
            value_s += jnp.where(
                same, value_f[at - j : at - j + TILE, :] * short_ref[2, j : j + 1, :], 0.0
            )
        product_f[TILE * tile : TILE * (tile + 1), :] = (
            (key_s * value_s).astype(jnp.bfloat16).astype(jnp.float32)
        )

    for tile in range(tiles):
        at = HALO + TILE * tile
        here = ids_f[at : at + TILE, :]
        query_s = query_f[16 + TILE * tile : 16 + TILE * (tile + 1), :] * short_ref[0, 0:1, :]
        for j in range(1, SHORT):
            same = ids_f[at - j : at - j + TILE, :] == here
            begin = 16 + TILE * tile - j
            query_s += jnp.where(
                same, query_f[begin : begin + TILE, :] * short_ref[0, j : j + 1, :], 0.0
            )

        def one_contig(contig, summed, tile=tile, here=here):
            contig = contig.astype(jnp.float32)
            reach = TILE + MEDIUM
            begin = TILE * tile
            masked_f[...] = jnp.where(
                ids_f[LEAD + begin : LEAD + begin + reach, :] == contig,
                product_f[begin : begin + reach, :],
                0.0,
            )
            total = jnp.zeros((TILE, LANES), jnp.float32)
            for r in range(8):
                shifted = masked_f[8 - r : 8 - r + reach - 8, :]
                for a in range(MEDIUM // 8):
                    total += (
                        taps_f[8 * a + r : 8 * a + r + 1, :]
                        * shifted[8 * (15 - a) : 8 * (15 - a) + TILE]
                    )
            return jnp.where(here == contig, total, summed)

        summed = lax.fori_loop(
            span[2 * tile],
            span[2 * tile + 1] + 1,
            one_contig,
            jnp.zeros((TILE, LANES), jnp.float32),
        )
        product = product_f[MEDIUM + TILE * tile : MEDIUM + TILE * (tile + 1), :]
        out_ref[TILE * tile : TILE * (tile + 1), :] = (
            query_s * (summed + skip_ref[...] * product)
        ).astype(jnp.bfloat16)


def pack_kernel(key, value, query, ids_ref, out, sem):
    copies = [
        pltpu.make_async_copy(key.at[512 - HALO : 512], out.at[0:HALO], sem.at[0]),
        pltpu.make_async_copy(value.at[512 - HALO : 512], out.at[HALO : 2 * HALO], sem.at[1]),
        pltpu.make_async_copy(
            query.at[512 - 16 : 512], out.at[2 * HALO : 2 * HALO + 16], sem.at[2]
        ),
    ]
    for copy in copies:
        copy.start()
    for i in range(4):
        row = ids_ref[i : i + 1, :].astype(jnp.float32)
        out[2 * HALO + 16 : PACK, LANES * i : LANES * (i + 1)] = jnp.broadcast_to(
            row, (16, LANES)
        ).astype(jnp.bfloat16)
    for copy in copies:
        copy.wait()


def pack_tail(key, value, query, ids):
    hbm = pl.BlockSpec(memory_space=pl.ANY)
    channels = key.shape[1]
    return pl.pallas_call(
        pack_kernel,
        out_shape=jax.ShapeDtypeStruct((PACK, channels), jnp.bfloat16),
        in_specs=[hbm, hbm, hbm, pl.BlockSpec(memory_space=pltpu.VMEM)],
        out_specs=pl.BlockSpec(memory_space=pltpu.VMEM),
        scratch_shapes=[pltpu.SemaphoreType.DMA((3,))],
        compiler_params=pltpu.CompilerParams(vmem_limit_bytes=60 << 20),
        cost_estimate=pl.CostEstimate(flops=0, bytes_accessed=700000, transcendentals=0),
        name="pack_tail",
    )(key, value, query, ids)


def gate(whole_gated, halo, query, key, value, ids, short_taps, medium_taps, decay, skip):
    late = whole_gated is None
    channels = query.shape[1]
    whole = lambda rows: pl.BlockSpec((rows, LANES), lambda i: (0, i))
    specs = [whole(512)] * 3 + [
        pl.BlockSpec((4, LANES), lambda i: (0, 0)),
        pl.BlockSpec((3, SHORT, LANES), lambda i: (0, 0, i)),
        whole(MEDIUM),
        whole(1),
        whole(1),
    ]
    args = [query, key, value, ids, short_taps, medium_taps, decay, skip]
    if not late:
        ids_block = (2 * HALO + 16) // 16
        specs = [pl.BlockSpec(memory_space=pl.ANY), whole(halo.shape[0]), pl.BlockSpec((16, channels), lambda i: (ids_block, 0))] + specs
        args = [whole_gated, halo, halo] + args
    f32 = lambda rows: pltpu.VMEM((rows, LANES), jnp.float32)
    return pl.pallas_call(
        functools.partial(filter_kernel, late),
        grid=(channels // LANES,),
        out_shape=jax.ShapeDtypeStruct((2 * HALF, channels), jnp.bfloat16),
        in_specs=specs,
        out_specs=pl.BlockSpec((HALF, LANES), lambda i: (int(late), i)),
        input_output_aliases={} if late else {0: 0},
        scratch_shapes=[
            f32(HALF + 16),
            f32(WINDOW),
            f32(WINDOW),
            f32(WINDOW),
            f32(PRODUCTS),
            f32(TILE + MEDIUM),
            f32(MEDIUM),
            pltpu.SMEM((2 * HALF // TILE,), jnp.int32),
        ],
        compiler_params=pltpu.CompilerParams(vmem_limit_bytes=60 << 20),
        cost_estimate=pl.CostEstimate(
            flops=2 * MEDIUM * HALF * channels * 4, bytes_accessed=2 << 20, transcendentals=65536
        ),
        name="gate_late" if late else "gate_early",
    )(*args)


def near_kernel(places, *refs):
    count = 2 * SIDE - 1
    panels = refs[:count]
    weight, total, far_weights, blocks, weights, block_sem, weight_sem = refs[count:]
    near = 2 * count
    copies = []
    for at in range(near):
        panel = panels[at // 2].at[at % 2]
        copies.append(
            (
                pltpu.make_async_copy(weight.at[places[at]], weights.at[at], weight_sem.at[at]),
                pltpu.make_async_copy(panel, blocks.at[at], block_sem.at[at]),
            )
        )
    later = [
        pltpu.make_async_copy(
            weight.at[places[near + i]], far_weights.at[i], weight_sem.at[near + i]
        )
        for i in range(2)
    ]
    for pair in copies:
        for copy in pair:
            copy.start()
    for copy in later:
        copy.start()
    for at in range(near):
        for copy in copies[at]:
            copy.wait()
        part = jnp.dot(blocks[at], weights[at], preferred_element_type=jnp.float32)
        total[...] = part if at == 0 else total[...] + part
    for copy in later:
        copy.wait()


def far_kernel(total, weights, panel, out_ref, blocks, rounded, sem, out_sem):
    tokens = total.shape[0]
    halves = [slice(tokens // 2 * half, tokens // 2 * (half + 1)) for half in range(2)]
    copies = [
        [
            pltpu.make_async_copy(panel.at[i, rows], blocks.at[i, rows], sem.at[2 * half + i])
            for i in range(2)
        ]
        for half, rows in enumerate(halves)
    ]
    for pair in copies:
        for copy in pair:
            copy.start()
    gives = []
    for half, rows in enumerate(halves):
        for copy in copies[half]:
            copy.wait()
        summed = total[rows]
        for i in range(2):
            summed += jnp.dot(blocks[i, rows], weights[i], preferred_element_type=jnp.float32)
        rounded[rows] = summed.astype(jnp.bfloat16)
        gives.append(pltpu.make_async_copy(rounded.at[rows], out_ref.at[rows], out_sem.at[half]))
        gives[half].start()
    for give in gives:
        give.wait()


def project(near, far, weight):
    chan = lax.axis_index("chan")
    y, x = chan // SIDE, chan % SIDE
    core = lax.axis_index("stretch") % 2
    outer = jnp.repeat(jnp.array(OFFSETS, jnp.int32), SIDE)
    inner = jnp.tile(jnp.array(OFFSETS, jnp.int32), SIDE)
    oy = jnp.where(core == 0, outer, inner)
    ox = jnp.where(core == 0, inner, outer)
    places = (y + oy + SIDE) % SIDE * SIDE + (x + ox + SIDE) % SIDE
    slots = SIDE * SIDE
    columns = weight.shape[1]
    tokens, depth = near[0].shape[1:]
    hbm = pl.BlockSpec(memory_space=pl.ANY)
    vmem = pl.BlockSpec(memory_space=pltpu.VMEM)
    params = pltpu.CompilerParams(vmem_limit_bytes=54 << 20)
    cost = lambda blocks: pl.CostEstimate(
        flops=2 * tokens * blocks * depth * columns, bytes_accessed=blocks << 20, transcendentals=0
    )
    count = slots - 2
    total, weights = pl.pallas_call(
        near_kernel,
        out_shape=[
            pltpu.VMEM((tokens, columns), jnp.float32),
            pltpu.VMEM((2, depth, columns), jnp.bfloat16),
        ],
        in_specs=[pl.BlockSpec(memory_space=pltpu.SMEM)] + [hbm] * (len(near) + 1),
        out_specs=[vmem, vmem],
        scratch_shapes=[
            pltpu.VMEM((count, tokens, depth), jnp.bfloat16),
            pltpu.VMEM((count, depth, columns), jnp.bfloat16),
            pltpu.SemaphoreType.DMA((count,)),
            pltpu.SemaphoreType.DMA((slots,)),
        ],
        compiler_params=params,
        cost_estimate=cost(count),
        name="project_near",
    )(places.astype(jnp.int32), *near, weight.reshape(slots, depth, columns))
    in_vmem = lambda value: pltpu.with_memory_space_constraint(value, pltpu.VMEM)
    return pl.pallas_call(
        far_kernel,
        out_shape=jax.ShapeDtypeStruct((tokens, columns), jnp.bfloat16),
        in_specs=[vmem, vmem, hbm],
        out_specs=hbm,
        scratch_shapes=[
            pltpu.VMEM((2, tokens, depth), jnp.bfloat16),
            pltpu.VMEM((tokens, columns), jnp.bfloat16),
            pltpu.SemaphoreType.DMA((4,)),
            pltpu.SemaphoreType.DMA((2,)),
        ],
        compiler_params=params,
        cost_estimate=cost(2),
        name="project_far",
    )(in_vmem(total), in_vmem(weights), far)


def body(
    query_in,
    key_in,
    value_in,
    contig_ids,
    short_taps,
    medium_taps,
    decay_rate,
    skip_gain,
    out_weight,
):
    weight = lax.all_gather(out_weight, "stretch", axis=0, tiled=True)
    rest = (
        query_in,
        key_in,
        value_in,
        contig_ids.reshape(-1, LANES),
        short_taps,
        medium_taps,
        decay_rate[None, :],
        skip_gain[None, :],
    )
    devices = lax.axis_size("stretch")
    pack = pack_tail(key_in, value_in, query_in, rest[3])
    halo = lax.ppermute(pack, "stretch", [(i, i + 1) for i in range(devices - 1)])
    gated = gate(None, None, *rest)
    gated = gate(gated, halo, *rest)
    line = [gated] + [first_way(gated, -by) for by in OFFSETS[1:]]
    low, high = jnp.stack(line[:2]), jnp.stack(line[2:])
    below_low = second_way(low, 1)
    above_high = second_way(high, -1)
    below_high = second_way(high, 1)
    above_low = second_way(low, -1)
    far_low = second_way(below_low, 1)
    far_high = second_way(above_high, -1)
    near = [low, high, below_low, below_high, above_low, above_high, far_low]
    return project(near, far_high, weight)


def solution(mesh):
    placed = (
        P("stretch", "chan"),
        P("stretch", "chan"),
        P("stretch", "chan"),
        P("stretch"),
        P(None, None, "chan"),
        P(None, "chan"),
        P("chan"),
        P("chan"),
        P("stretch", "chan"),
    )
    return jax.shard_map(
        body, mesh=mesh, in_specs=placed, out_specs=P("stretch", "chan"), check_vma=False
    )
```

```python
import functools

import jax
import jax.numpy as jnp
from jax import lax
from jax.experimental import pallas as pl
from jax.experimental.pallas import tpu as pltpu
from jax.sharding import PartitionSpec as P

MEDIUM = 128
SHORT = 7
SIDE = 4
HALO = 144
HALF = 256
WINDOW = HALO + HALF
PACK = 2 * HALO + 16 + 16
LEAD = 16
PRODUCTS = WINDOW - LEAD
TILE = 64
LANES = 128
OFFSETS = (0, -1, 1, 2)


def first_way(value, by):
    return lax.ppermute(value, ("chan", "stretch"), moves(by, 0))


def second_way(value, by):
    return lax.ppermute(value, ("chan", "stretch"), moves(by, 1))


def moves(by, way):
    stretch = lax.axis_size("stretch")
    pairs = []
    for y in range(SIDE):
        for x in range(SIDE):
            for place in range(stretch):
                if place % 2 == way:
                    to = y * SIDE + (x + by) % SIDE
                else:
                    to = (y + by) % SIDE * SIDE + x
                pairs.append(((y * SIDE + x) * stretch + place, to * stretch + place))
    return pairs


def id_column(row):
    return jnp.broadcast_to(row, (LANES, LANES)).T


def filter_kernel(late, *refs):
    if late:
        halo_ref = halo_ids_ref = None
    else:
        _, halo_ref, halo_ids_ref, *refs = refs
    (query_ref, key_ref, value_ref, ids_ref, short_ref, medium_ref, decay_ref, skip_ref) = refs[:8]
    out_ref, query_f, key_f, value_f, ids_f, product_f, masked_f, taps_f, span = refs[8:]
    tiles = HALF // TILE

    @pl.when(pl.program_id(0) == 0)
    def _():
        own = [id_column(ids_ref[i : i + 1, :].astype(jnp.float32)) for i in range(4)]
        if late:
            ids_f[0:16, :] = own[0][112:128]
            for i in range(1, 4):
                ids_f[16 + 128 * (i - 1) : 16 + 128 * i, :] = own[i]
        else:
            before = [
                id_column(halo_ids_ref[0:1, 128 * i : 128 * i + 128].astype(jnp.float32))
                for i in (2, 3)
            ]
            ids_f[0:16, :] = before[0][112:128]
            ids_f[16:144, :] = before[1]
            ids_f[144:272, :] = own[0]
            ids_f[272:400, :] = own[1]
        for tile in range(tiles):
            rows = ids_f[HALO + TILE * tile : HALO + TILE * (tile + 1), :]
            span[2 * tile] = jnp.min(rows).astype(jnp.int32)
            span[2 * tile + 1] = jnp.max(rows).astype(jnp.int32)

    if late:
        first = 512 - WINDOW
        key_f[...] = key_ref[first:, :].astype(jnp.float32)
        value_f[...] = value_ref[first:, :].astype(jnp.float32)
        query_f[...] = query_ref[512 - HALF - 16 :, :].astype(jnp.float32)
    else:
        key_f[0:HALO, :] = halo_ref[0:HALO, :].astype(jnp.float32)
        key_f[HALO:, :] = key_ref[0:HALF, :].astype(jnp.float32)
        value_f[0:HALO, :] = halo_ref[HALO : 2 * HALO, :].astype(jnp.float32)
        value_f[HALO:, :] = value_ref[0:HALF, :].astype(jnp.float32)
        query_f[0:16, :] = halo_ref[2 * HALO : 2 * HALO + 16, :].astype(jnp.float32)
        query_f[16:, :] = query_ref[0:HALF, :].astype(jnp.float32)

    lag = lax.broadcasted_iota(jnp.int32, (MEDIUM, LANES), 0).astype(jnp.float32)
    taps_f[...] = medium_ref[...] * jnp.exp(-decay_ref[...] * lag)

    for tile in range(PRODUCTS // TILE):
        at = LEAD + TILE * tile
        here = ids_f[at : at + TILE, :]
        key_s = key_f[at : at + TILE, :] * short_ref[1, 0:1, :]
        value_s = value_f[at : at + TILE, :] * short_ref[2, 0:1, :]
        for j in range(1, SHORT):
            same = ids_f[at - j : at - j + TILE, :] == here
            key_s += jnp.where(same, key_f[at - j : at - j + TILE, :] * short_ref[1, j : j + 1, :], 0.0)
            value_s += jnp.where(
                same, value_f[at - j : at - j + TILE, :] * short_ref[2, j : j + 1, :], 0.0
            )
        product_f[TILE * tile : TILE * (tile + 1), :] = (
            (key_s * value_s).astype(jnp.bfloat16).astype(jnp.float32)
        )

    for tile in range(tiles):
        at = HALO + TILE * tile
        here = ids_f[at : at + TILE, :]
        query_s = query_f[16 + TILE * tile : 16 + TILE * (tile + 1), :] * short_ref[0, 0:1, :]
        for j in range(1, SHORT):
            same = ids_f[at - j : at - j + TILE, :] == here
            begin = 16 + TILE * tile - j
            query_s += jnp.where(
                same, query_f[begin : begin + TILE, :] * short_ref[0, j : j + 1, :], 0.0
            )

        def one_contig(contig, summed, tile=tile, here=here):
            contig = contig.astype(jnp.float32)
            reach = TILE + MEDIUM
            begin = TILE * tile
            masked_f[...] = jnp.where(
                ids_f[LEAD + begin : LEAD + begin + reach, :] == contig,
                product_f[begin : begin + reach, :],
                0.0,
            )
            total = jnp.zeros((TILE, LANES), jnp.float32)
            for r in range(8):
                shifted = masked_f[8 - r : 8 - r + reach - 8, :]
                for a in range(MEDIUM // 8):
                    total += (
                        taps_f[8 * a + r : 8 * a + r + 1, :]
                        * shifted[8 * (15 - a) : 8 * (15 - a) + TILE]
                    )
            return jnp.where(here == contig, total, summed)

        summed = lax.fori_loop(
            span[2 * tile],
            span[2 * tile + 1] + 1,
            one_contig,
            jnp.zeros((TILE, LANES), jnp.float32),
        )
        product = product_f[MEDIUM + TILE * tile : MEDIUM + TILE * (tile + 1), :]
        out_ref[TILE * tile : TILE * (tile + 1), :] = (
            query_s * (summed + skip_ref[...] * product)
        ).astype(jnp.bfloat16)


def pack_kernel(key, value, query, ids_ref, out, sem):
    copies = [
        pltpu.make_async_copy(key.at[512 - HALO : 512], out.at[0:HALO], sem.at[0]),
        pltpu.make_async_copy(value.at[512 - HALO : 512], out.at[HALO : 2 * HALO], sem.at[1]),
        pltpu.make_async_copy(
            query.at[512 - 16 : 512], out.at[2 * HALO : 2 * HALO + 16], sem.at[2]
        ),
    ]
    for copy in copies:
        copy.start()
    for i in range(4):
        row = ids_ref[i : i + 1, :].astype(jnp.float32)
        out[2 * HALO + 16 : PACK, LANES * i : LANES * (i + 1)] = jnp.broadcast_to(
            row, (16, LANES)
        ).astype(jnp.bfloat16)
    for copy in copies:
        copy.wait()


def pack_tail(key, value, query, ids):
    hbm = pl.BlockSpec(memory_space=pl.ANY)
    channels = key.shape[1]
    return pl.pallas_call(
        pack_kernel,
        out_shape=jax.ShapeDtypeStruct((PACK, channels), jnp.bfloat16),
        in_specs=[hbm, hbm, hbm, pl.BlockSpec(memory_space=pltpu.VMEM)],
        out_specs=pl.BlockSpec(memory_space=pltpu.VMEM),
        scratch_shapes=[pltpu.SemaphoreType.DMA((3,))],
        compiler_params=pltpu.CompilerParams(vmem_limit_bytes=60 << 20),
        cost_estimate=pl.CostEstimate(flops=0, bytes_accessed=700000, transcendentals=0),
        name="pack_tail",
    )(key, value, query, ids)


def gate(whole_gated, halo, query, key, value, ids, short_taps, medium_taps, decay, skip):
    late = whole_gated is None
    channels = query.shape[1]
    whole = lambda rows: pl.BlockSpec((rows, LANES), lambda i: (0, i))
    specs = [whole(512)] * 3 + [
        pl.BlockSpec((4, LANES), lambda i: (0, 0)),
        pl.BlockSpec((3, SHORT, LANES), lambda i: (0, 0, i)),
        whole(MEDIUM),
        whole(1),
        whole(1),
    ]
    args = [query, key, value, ids, short_taps, medium_taps, decay, skip]
    if not late:
        ids_block = (2 * HALO + 16) // 16
        specs = [pl.BlockSpec(memory_space=pl.ANY), whole(halo.shape[0]), pl.BlockSpec((16, channels), lambda i: (ids_block, 0))] + specs
        args = [whole_gated, halo, halo] + args
    f32 = lambda rows: pltpu.VMEM((rows, LANES), jnp.float32)
    return pl.pallas_call(
        functools.partial(filter_kernel, late),
        grid=(channels // LANES,),
        out_shape=jax.ShapeDtypeStruct((2 * HALF, channels), jnp.bfloat16),
        in_specs=specs,
        out_specs=pl.BlockSpec((HALF, LANES), lambda i: (int(late), i)),
        input_output_aliases={} if late else {0: 0},
        scratch_shapes=[
            f32(HALF + 16),
            f32(WINDOW),
            f32(WINDOW),
            f32(WINDOW),
            f32(PRODUCTS),
            f32(TILE + MEDIUM),
            f32(MEDIUM),
            pltpu.SMEM((2 * HALF // TILE,), jnp.int32),
        ],
        compiler_params=pltpu.CompilerParams(vmem_limit_bytes=60 << 20),
        cost_estimate=pl.CostEstimate(
            flops=2 * MEDIUM * HALF * channels * 4, bytes_accessed=2 << 20, transcendentals=65536
        ),
        name="gate_late" if late else "gate_early",
    )(*args)


def near_kernel(places, *refs):
    count = 2 * SIDE - 1
    panels = refs[:count]
    weight, total, blocks, weights, block_sem, weight_sem = refs[count:]
    near = 2 * count
    copies = []
    for at in range(near):
        panel = panels[at // 2].at[at % 2]
        copies.append(
            (
                pltpu.make_async_copy(weight.at[places[at]], weights.at[at], weight_sem.at[at]),
                pltpu.make_async_copy(panel, blocks.at[at], block_sem.at[at]),
            )
        )
    for pair in copies:
        for copy in pair:
            copy.start()
    for at in range(near):
        for copy in copies[at]:
            copy.wait()
        part = jnp.dot(blocks[at], weights[at], preferred_element_type=jnp.float32)
        total[...] = part if at == 0 else total[...] + part


def far_kernel(places, total, panel, weight, out_ref, blocks, weights, rounded, sem, out_sem):
    first = 4 * SIDE - 2
    copies = [pltpu.make_async_copy(panel.at[i], blocks.at[i], sem.at[i]) for i in range(2)] + [
        pltpu.make_async_copy(weight.at[places[first + i]], weights.at[i], sem.at[2 + i])
        for i in range(2)
    ]
    for copy in copies:
        copy.start()
    for copy in copies:
        copy.wait()
    tokens = total.shape[0]
    gives = []
    for half in range(2):
        rows = slice(tokens // 2 * half, tokens // 2 * (half + 1))
        summed = total[rows]
        for i in range(2):
            summed += jnp.dot(blocks[i, rows], weights[i], preferred_element_type=jnp.float32)
        rounded[rows] = summed.astype(jnp.bfloat16)
        gives.append(pltpu.make_async_copy(rounded.at[rows], out_ref.at[rows], out_sem.at[half]))
        gives[half].start()
    for give in gives:
        give.wait()


def project(near, far, weight):
    chan = lax.axis_index("chan")
    y, x = chan // SIDE, chan % SIDE
    core = lax.axis_index("stretch") % 2
    outer = jnp.repeat(jnp.array(OFFSETS, jnp.int32), SIDE)
    inner = jnp.tile(jnp.array(OFFSETS, jnp.int32), SIDE)
    oy = jnp.where(core == 0, outer, inner)
    ox = jnp.where(core == 0, inner, outer)
    places = (y + oy + SIDE) % SIDE * SIDE + (x + ox + SIDE) % SIDE
    slots = SIDE * SIDE
    columns = weight.shape[1]
    tokens, depth = near[0].shape[1:]
    hbm = pl.BlockSpec(memory_space=pl.ANY)
    vmem = pl.BlockSpec(memory_space=pltpu.VMEM)
    params = pltpu.CompilerParams(vmem_limit_bytes=54 << 20)
    cost = lambda blocks: pl.CostEstimate(
        flops=2 * tokens * blocks * depth * columns, bytes_accessed=blocks << 20, transcendentals=0
    )
    count = slots - 2
    places = places.astype(jnp.int32)
    weight = weight.reshape(slots, depth, columns)
    total = pl.pallas_call(
        near_kernel,
        out_shape=pltpu.VMEM((tokens, columns), jnp.float32),
        in_specs=[pl.BlockSpec(memory_space=pltpu.SMEM)] + [hbm] * (len(near) + 1),
        out_specs=vmem,
        scratch_shapes=[
            pltpu.VMEM((count, tokens, depth), jnp.bfloat16),
            pltpu.VMEM((count, depth, columns), jnp.bfloat16),
            pltpu.SemaphoreType.DMA((count,)),
            pltpu.SemaphoreType.DMA((slots,)),
        ],
        compiler_params=params,
        cost_estimate=cost(count),
        name="project_near",
    )(places, *near, weight)
    in_vmem = lambda value: pltpu.with_memory_space_constraint(value, pltpu.VMEM)
    return pl.pallas_call(
        far_kernel,
        out_shape=jax.ShapeDtypeStruct((tokens, columns), jnp.bfloat16),
        in_specs=[pl.BlockSpec(memory_space=pltpu.SMEM), vmem, hbm, hbm],
        out_specs=hbm,
        scratch_shapes=[
            pltpu.VMEM((2, tokens, depth), jnp.bfloat16),
            pltpu.VMEM((2, depth, columns), jnp.bfloat16),
            pltpu.VMEM((tokens, columns), jnp.bfloat16),
            pltpu.SemaphoreType.DMA((4,)),
            pltpu.SemaphoreType.DMA((2,)),
        ],
        compiler_params=params,
        cost_estimate=cost(2),
        name="project_far",
    )(places, in_vmem(total), far, weight)


def body(
    query_in,
    key_in,
    value_in,
    contig_ids,
    short_taps,
    medium_taps,
    decay_rate,
    skip_gain,
    out_weight,
):
    weight = lax.all_gather(out_weight, "stretch", axis=0, tiled=True)
    rest = (
        query_in,
        key_in,
        value_in,
        contig_ids.reshape(-1, LANES),
        short_taps,
        medium_taps,
        decay_rate[None, :],
        skip_gain[None, :],
    )
    devices = lax.axis_size("stretch")
    pack = pack_tail(key_in, value_in, query_in, rest[3])
    halo = lax.ppermute(pack, "stretch", [(i, i + 1) for i in range(devices - 1)])
    gated = gate(None, None, *rest)
    gated = gate(gated, halo, *rest)
    line = [gated] + [first_way(gated, -by) for by in OFFSETS[1:]]
    low, high = jnp.stack(line[:2]), jnp.stack(line[2:])
    below_low = second_way(low, 1)
    above_high = second_way(high, -1)
    below_high = second_way(high, 1)
    above_low = second_way(low, -1)
    far_low = second_way(below_low, 1)
    far_high = second_way(above_high, -1)
    near = [low, high, below_low, below_high, above_low, above_high, far_low]
    return project(near, far_high, weight)


def solution(mesh):
    placed = (
        P("stretch", "chan"),
        P("stretch", "chan"),
        P("stretch", "chan"),
        P("stretch"),
        P(None, None, "chan"),
        P(None, "chan"),
        P("chan"),
        P("chan"),
        P("stretch", "chan"),
    )
    return jax.shard_map(
        body, mesh=mesh, in_specs=placed, out_specs=P("stretch", "chan"), check_vma=False
    )
```
